32 devices in a mesh: ctx: 16 (over z, x, core), exp: 2 (over y).
Axes of the slice: x: 2, y: 2, z: 4, core: 2. Of those that a mesh axis runs over, the one named last changes fastest.
Arguments:
- hidden_in: bfloat16 [4096, 2048], P(('ctx', 'exp')), may hold values from -6 to 6
- queries: bfloat16 [4096, 4096], P('ctx', 'exp'), may hold values from -400 to 400
- keys: bfloat16 [4096, 512], P('ctx'), may hold values from -8 to 8
- values: bfloat16 [4096, 512], P('ctx'), may hold values from -6 to 6
- blocks: int32 [32, 8], P('ctx'), may hold values from 0 to 31, as said below
- out_weight: bfloat16 [4096, 2048], P('exp'), may hold values from -0.75 to 0.75
- norm_gain: float32 [2048], replicated, may hold values from 0.1 to 1.9
- w_gate_up: bfloat16 [8, 2048, 1536], P('exp'), may hold values from -0.125 to 0.125
- w_down: bfloat16 [8, 768, 2048], P('exp'), may hold values from -0.21875 to 0.21875
- expert_ids: int32 [4096, 2], P(('ctx', 'exp')), may hold values from 0 to 7, all different within a row; in each aligned block of 128 rows (0 to 127, 128 to 255, ...) at most 64 rows name the same one
- gate_weights: float32 [4096, 2], P(('ctx', 'exp')), may hold values from 0.25 to 1
Outputs:
- layer_out: bfloat16 [4096, 2048], P(('ctx', 'exp'))
The draws below stay inside these ranges and needn't reach their ends.
Inputs may be any that keep to these rules, and one draw needn't show every extreme that they name: Row b lists key blocks for query block b: its first entry is b, every entry lies in 0 to b, and entries may repeat. `expert_ids`: A token's 2 experts are distinct. Within the 128 rows of one device (aligned blocks of rows), no expert is named more than 64 times, a bound that some block reaches.
All inputs are finite; a program needn't handle non-finite values.
Results may differ from the reference program's by a relative error of at most 0.019.
Values may be sent and summed in bfloat16 or wider, within the bound.
A program may use at most 128 MiB of HBM per device.

```python
import math
import jax
import jax.numpy as jnp
import numpy as np
from jax import lax

D = 2048
HQ = 32
KVH = 4
HD = 128
FF = 768
BLK = 128
KSEL = 8
TOP = 2
SEQ = 4096
NBLK = 32
TOK_DEV = 128
CAP = 64
EXPERTS = 8
N_CTX = 16
N_EXP = 2


def paired_fields(key):
    base_key = jax.random.fold_in(key, 4242)
    query_key, key_key = jax.random.split(base_key, 2)
    query_field = jnp.clip(jax.random.normal(query_key, (SEQ, HQ * HD), jnp.float32), -6.0, 6.0)
    key_field = jnp.clip(jax.random.normal(key_key, (SEQ, KVH * HD), jnp.float32), -6.0, 6.0)
    return (query_field, key_field)


def draw_queries(key, part):
    return paired_fields(key)[0].astype(jnp.bfloat16)


def draw_keys(key, part):
    return paired_fields(key)[1].astype(jnp.bfloat16)


def draw_blocks(key, part):
    block_row = jnp.arange(NBLK, dtype=jnp.int32)[:, None]
    raw_draw = jax.random.randint(jax.random.fold_in(key, 77), (NBLK, KSEL), 0, 1 << 30, dtype=jnp.int32)
    picked = raw_draw % (block_row + 1)
    column = jnp.arange(KSEL, dtype=jnp.int32)[None, :]
    return jnp.where(column == 0, block_row, picked).astype(jnp.int32)


def levels(own_key, extent, pieces, smallest, largest):
    gain = 1.0
    for dim, parts in pieces:
        draws = jax.random.uniform(jax.random.fold_in(jax.random.fold_in(own_key, 6), dim), (parts,), jnp.float32, smallest / len(pieces), largest / len(pieces))
        gain = gain * jnp.repeat(jnp.exp(draws), extent[dim] // parts).reshape((-1,) + (1,) * (len(extent) - 1 - dim))
    return gain


def deal_out(stream_key, own, number, rows, count, top, most, skew):
    order = jax.random.permutation(stream_key, count)
    crowded, common = shares(count, rows * top, most, skew, True), shares(count, rows * top, most, skew, False)
    places = jnp.arange(count)

    def named(sizes, offset_by):
        used = int((sizes > 0).sum())
        fixed = max(1, used // 4)
        shifted = fixed + (places - fixed + offset_by * (used - fixed)) % max(1, count - fixed)
        return jnp.zeros((count,), jnp.int32).at[order[jnp.where(places < fixed, places, shifted)]].set(jnp.asarray(sizes, jnp.int32))

    sizes = jnp.where(number % 4 == 0, named(crowded, number // 4), named(common, number - number // 4 - 1))
    mixed = jax.random.permutation(jax.random.fold_in(own, 3), count)
    source_of, receiver = mixed[0:count // 2 * 2:2], mixed[1:count // 2 * 2:2]
    room = jnp.minimum(sizes[source_of] - 1, most - sizes[receiver]) // 2
    room = jnp.where((source_of == order[0]) | (receiver == order[0]) | (sizes[receiver] == 0), 0, jnp.maximum(room, 0))
    shifted = jax.random.randint(jax.random.fold_in(own, 4), (count // 2,), 0, 1 << 20) % (room + 1)
    sizes = sizes.at[source_of].add(-shifted).at[receiver].add(shifted)
    members = jnp.searchsorted(jnp.cumsum(sizes), jnp.arange(rows * top), side="right").astype(jnp.int32)
    table = members.reshape(top, rows).T
    table = table[jax.random.permutation(jax.random.fold_in(own, 1), rows)]
    offset_by = jax.random.randint(jax.random.fold_in(own, 2), (rows, 1), 0, top)
    return jnp.take_along_axis(table, (jnp.arange(top)[None, :] + offset_by) % top, axis=1)


def shares(number_of, total, bound, lean, full):
    portions = [(1 << 20) // math.isqrt(standing ** lean) + 1 for standing in range(1, number_of + 1)]
    largest = bound if full else min(bound, max(-(-total // number_of), total * portions[0] // sum(portions)))
    least = 1 if total - largest >= number_of - 1 else 0
    given, spare = [largest] + [least] * (number_of - 1), total - largest - least * (number_of - 1)
    while spare > 0:
        movable = [i for i in range(1, number_of) if given[i] < largest] or [i for i in range(1, number_of) if given[i] < bound]
        whole, budget = sum([portions[i] for i in movable]), spare
        for i in movable:
            extra = min(bound - given[i], max(1, budget * portions[i] // whole), spare)
            given[i] = given[i] + extra
            spare = spare - extra
    return np.array(given)


def gaussian(rng, extent, width, bound, cuts=(), held_as=jnp.bfloat16):
    factor_of = levels(rng, extent, cuts, -0.22, 0.18) if cuts else 1.0
    drawn = jax.random.normal(rng, extent, jnp.float32) * width * factor_of
    return jnp.minimum(jnp.maximum(drawn, -bound), bound).astype(held_as)


def setup_inputs(seed: int = 0) -> dict:
    key_of = jax.random.split(jax.random.key(seed), 12)
    hidden_in = gaussian(key_of[0], (SEQ, D), 1.0, 6.0, ((0, 32),))
    queries = draw_queries(jax.random.fold_in(key_of[11], 71), 0)
    keys = draw_keys(jax.random.fold_in(key_of[11], 71), 0)
    values = gaussian(key_of[3], (SEQ, KVH * HD), 1.0, 6.0, ((0, 16),))
    blocks = draw_blocks(jax.random.fold_in(key_of[11], 71), 0)
    out_weight = gaussian(key_of[5], (HQ * HD, D), 64 ** -0.5, 0.75, ((0, 2),))
    norm_gain = jnp.clip(1.0 + 0.18 * jax.random.normal(key_of[6], (D,), jnp.float32), 0.1, 1.9)
    w_gate_up = gaussian(key_of[7], (EXPERTS, D, 2 * FF), D ** -0.5, 0.125, ((0, 2),))
    w_down = gaussian(key_of[8], (EXPERTS, FF, D), FF ** -0.5, 0.21875, ((0, 2),))
    expert_ids_keys = jax.random.split(jax.random.fold_in(key_of[9], 1), SEQ // TOK_DEV)
    expert_ids_turns = jax.random.permutation(jax.random.fold_in(key_of[9], 3), SEQ // TOK_DEV)
    expert_ids = jax.vmap(lambda own, number: deal_out(jax.random.fold_in(key_of[9], 2), own, number, TOK_DEV, EXPERTS, TOP, CAP, 2))(expert_ids_keys, expert_ids_turns).reshape((SEQ, TOP))
    gate_weights = jnp.clip(0.25 + 0.75 * jax.random.uniform(key_of[10], (SEQ, TOP), jnp.float32) ** levels(key_of[10], (SEQ, TOP), ((0, 32),), -0.2, 0.2), 0.25, 1.0)
    return dict(hidden_in=hidden_in, queries=queries, keys=keys, values=values, blocks=blocks, out_weight=out_weight, norm_gain=norm_gain, w_gate_up=w_gate_up, w_down=w_down, expert_ids=expert_ids, gate_weights=gate_weights)


NEG_FILL = -1e+30

def attention(queries, keys, values, blocks):
    head_group = HQ // KVH
    score_scale = 1.0 / math.sqrt(HD)
    query_tiles = queries.reshape(NBLK, BLK, KVH, head_group, HD)
    key_tiles = keys.reshape(NBLK, BLK, KVH, HD)
    value_tiles = values.reshape(NBLK, BLK, KVH, HD)
    slot_index = jnp.arange(KSEL, dtype=jnp.int32)
    inner_pos = jnp.arange(BLK, dtype=jnp.int32)

    def one_block(index):
        listing = blocks[index]
        earlier = slot_index[None, :] < slot_index[:, None]
        repeated = jnp.any((listing[:, None] == listing[None, :]) & earlier, axis=1)
        key_rows = key_tiles[listing].reshape(KSEL * BLK, KVH, HD).astype(jnp.float32)
        value_rows = value_tiles[listing].reshape(KSEL * BLK, KVH, HD).astype(jnp.float32)
        query_rows = query_tiles[index].astype(jnp.float32)
        scores = jnp.einsum('skgd,tkd->skgt', query_rows, key_rows) * score_scale
        query_pos = index * BLK + inner_pos
        key_pos = (listing[:, None] * BLK + inner_pos[None, :]).reshape(KSEL * BLK)
        fresh = jnp.broadcast_to(jnp.logical_not(repeated)[:, None], (KSEL, BLK)).reshape(KSEL * BLK)
        live = fresh[None, :] & (key_pos[None, :] <= query_pos[:, None])
        live_full = live[:, None, None, :]
        top_score = lax.optimization_barrier(jnp.max(jnp.where(live_full, scores, NEG_FILL), axis=-1, keepdims=True))
        weights = jnp.where(live_full, jnp.exp(scores - top_score), 0.0)
        norm_sum = lax.optimization_barrier(jnp.sum(weights, axis=-1))
        rounded = lax.optimization_barrier(weights.astype(jnp.bfloat16)).astype(jnp.float32)
        mixed = jnp.einsum('skgt,tkd->skgd', rounded, value_rows)
        return (mixed / norm_sum[..., None]).astype(jnp.bfloat16).reshape(BLK, HQ * HD)
    tiles = lax.map(one_block, jnp.arange(NBLK, dtype=jnp.int32))
    return tiles.reshape(SEQ, HQ * HD)

def apply_experts(normed, expert_ids, w_gate_up, w_down):
    chosen = expert_ids.reshape(SEQ * TOP).astype(jnp.int32)
    flat_rows = jnp.repeat(normed, TOP, axis=0)
    order = jnp.argsort(chosen, stable=True).astype(jnp.int32)
    counts = lax.optimization_barrier(jnp.sum((chosen[:, None] == jnp.arange(EXPERTS, dtype=jnp.int32)[None, :]).astype(jnp.int32), axis=0))
    starts = (jnp.cumsum(counts) - counts).astype(jnp.int32)
    limit = CAP * N_CTX * N_EXP
    ordered = jnp.concatenate([flat_rows[order], jnp.zeros((limit, D), normed.dtype)], axis=0)
    row_index = jnp.arange(limit, dtype=jnp.int32)[:, None]

    def visit(expert, result):
        begin = starts[expert]
        rows_in = lax.dynamic_slice_in_dim(ordered, begin, limit, 0)
        gate_up = jnp.dot(rows_in, w_gate_up[expert], preferred_element_type=jnp.float32)
        acted = (jax.nn.silu(gate_up[:, :FF]) * gate_up[:, FF:]).astype(jnp.bfloat16)
        produced = jnp.dot(acted, w_down[expert], preferred_element_type=jnp.float32).astype(jnp.bfloat16)
        previous = lax.dynamic_slice_in_dim(result, begin, limit, 0)
        kept = jnp.where(row_index < counts[expert], produced, previous)
        return lax.dynamic_update_slice_in_dim(result, kept, begin, 0)
    result = lax.fori_loop(0, EXPERTS, visit, jnp.zeros((SEQ * TOP + limit, D), jnp.bfloat16))
    placed = jnp.zeros((SEQ * TOP, D), jnp.bfloat16).at[order].set(result[:SEQ * TOP])
    return placed.reshape(SEQ, TOP, D)

def reference(hidden_in, queries, keys, values, blocks, out_weight, norm_gain, w_gate_up, w_down, expert_ids, gate_weights):
    attended = attention(queries, keys, values, blocks)
    hidden = (hidden_in.astype(jnp.float32) + jnp.dot(attended, out_weight, preferred_element_type=jnp.float32)).astype(jnp.bfloat16)
    hidden_f = lax.optimization_barrier(hidden).astype(jnp.float32)
    mean_square = lax.optimization_barrier(jnp.mean(hidden_f * hidden_f, axis=-1, keepdims=True))
    normed = (hidden_f * lax.rsqrt(mean_square + 1e-06) * norm_gain).astype(jnp.bfloat16)
    expert_out = apply_experts(normed, expert_ids, w_gate_up, w_down)
    weighted = lax.optimization_barrier(jnp.sum(gate_weights[:, :, None] * expert_out.astype(jnp.float32), axis=1))
    return (hidden_f + weighted).astype(jnp.bfloat16)
```

```python
import math

import jax
import jax.numpy as jnp
from jax import lax
from jax.experimental import pallas as pl
from jax.experimental.pallas import tpu as pltpu
from jax.sharding import PartitionSpec as P

HQ = 32
KVH = 4
HD = 128
FF = 768
BLK = 128


NEG_FILL = -1e30


def shifted(value, axis, steps):
    count = lax.axis_size(axis)
    first, last = (max(0, -steps), min(count, count - steps))
    return lax.ppermute(value, axis, [(source, source + steps) for source in range(first, last)])


def body(
    hidden_in,
    queries,
    keys,
    values,
    blocks,
    out_weight,
    norm_gain,
    w_gate_up,
    w_down,
    expert_ids,
    gate_weights,
):
    query_len = queries.shape[0]
    local_heads = queries.shape[1] // HD
    head_group = HQ // KVH
    local_group = min(head_group, local_heads)
    kv_local = local_heads // local_group
    kv_width = kv_local * HD
    first_kv = lax.axis_index("exp") * local_heads // head_group
    kv_mine = jnp.concatenate(
        [
            lax.dynamic_slice_in_dim(keys, first_kv * HD, kv_width, 1),
            lax.dynamic_slice_in_dim(values, first_kv * HD, kv_width, 1),
        ],
        axis=1,
    )
    cycle_size = lax.axis_size("ctx")
    ctx_place = lax.axis_index("ctx")
    query_start = ctx_place * query_len
    score_scale = 1.0 / math.sqrt(HD)
    query_heads = queries.reshape(query_len, kv_local, local_group, HD)
    query_pos = query_start + jnp.arange(query_len, dtype=jnp.int32)
    query_tiles = blocks.shape[0]

    def update(state, key_part, value_part, live):
        running_max, weight_sum, accumulated = state
        row_count = key_part.shape[0]
        scores = (
            jnp.einsum(
                "skgd,tkd->skgt",
                query_heads,
                key_part.reshape(row_count, kv_local, HD),
                preferred_element_type=jnp.float32,
            )
            * score_scale
        )
        live_full = live[:, None, None, :]
        new_max = jnp.maximum(running_max, jnp.max(jnp.where(live_full, scores, NEG_FILL), axis=-1))
        weights = jnp.where(live_full, jnp.exp(scores - new_max[..., None]), 0.0)
        shrink = jnp.exp(running_max - new_max)
        weight_sum = weight_sum * shrink + jnp.sum(weights, axis=-1)
        product = jnp.einsum(
            "skgt,tkd->skgd",
            weights.astype(jnp.bfloat16),
            value_part.reshape(row_count, kv_local, HD),
            preferred_element_type=jnp.float32,
        )
        accumulated = accumulated * shrink[..., None] + product
        return (new_max, weight_sum, accumulated)

    def attend_block(state, kv_part, row_start):
        row_count = kv_part.shape[0]
        key_part = kv_part[:, :kv_width]
        value_part = kv_part[:, kv_width:]
        key_pos = row_start + jnp.arange(row_count, dtype=jnp.int32)
        listed = jnp.any(blocks[:, :, None] == (key_pos // BLK)[None, None, :], axis=1)
        listed_rows = jnp.broadcast_to(listed[:, None, :], (query_tiles, BLK, row_count)).reshape(
            query_len, row_count
        )
        live = listed_rows & (key_pos[None, :] <= query_pos[:, None])
        result_state = update(state, key_part, value_part, live)
        return result_state

    def attend(state, kv_part, row_start):
        row_count = kv_part.shape[0]
        return attend_block(state, kv_part, row_start)

    empty_state = (
        jnp.full((query_len, kv_local, local_group), NEG_FILL, jnp.float32),
        jnp.zeros((query_len, kv_local, local_group), jnp.float32),
        jnp.zeros((query_len, kv_local, local_group, HD), jnp.float32),
    )
    first_state = attend(empty_state, kv_mine, query_start)

    def cycle_turn(turn, carried):
        acc_state, travelling = carried
        travelling = shifted(travelling, "ctx", 1)
        source = (ctx_place - turn - 1) % cycle_size
        return (attend(acc_state, travelling, source * query_len), travelling)

    final_state, unused_kv = lax.fori_loop(0, cycle_size - 1, cycle_turn, (first_state, kv_mine))
    running_max, weight_sum, accumulated = final_state
    attended = (
        (accumulated / weight_sum[..., None])
        .astype(jnp.bfloat16)
        .reshape(query_len, local_heads * HD)
    )
    token_count = hidden_in.shape[0]
    mixed = lax.psum_scatter(
        jnp.dot(attended, out_weight, preferred_element_type=jnp.float32).astype(jnp.bfloat16),
        "exp",
        scatter_dimension=0,
        tiled=True,
    ).astype(jnp.float32)
    hidden = (hidden_in.astype(jnp.float32) + mixed).astype(jnp.bfloat16)
    hidden_f = lax.optimization_barrier(hidden).astype(jnp.float32)
    mean_square = jnp.mean(hidden_f * hidden_f, axis=-1, keepdims=True)
    normed = (hidden_f * lax.rsqrt(mean_square + 1e-06) * norm_gain).astype(jnp.bfloat16)
    exp_size = lax.axis_size("exp")
    local_experts = w_gate_up.shape[0]
    expert_total = local_experts * exp_size
    capacity = token_count // 2
    model_width = normed.shape[1]
    route_count = expert_ids.shape[1]
    flat_ids = expert_ids.reshape(token_count * route_count)
    flat_count = flat_ids.shape[0]
    order = jnp.arange(flat_count, dtype=jnp.int32)
    ahead = (flat_ids[:, None] == flat_ids[None, :]) & (order[None, :] < order[:, None])
    slot_rank = jnp.sum(ahead.astype(jnp.int32), axis=1)
    target = (flat_ids * capacity + slot_rank).reshape(token_count, route_count)
    slot_ids = jnp.arange(expert_total * capacity, dtype=jnp.int32)
    picks = target[:, :, None] == slot_ids[None, None, :]
    dispatch = jnp.any(picks, axis=1).astype(jnp.bfloat16)
    outgoing = (
        lax.dot_general(
            dispatch, normed, (((0,), (0,)), ((), ())), preferred_element_type=jnp.float32
        )
        .astype(jnp.bfloat16)
        .reshape(expert_total, capacity, model_width)
    )
    arrived = lax.all_to_all(outgoing, "exp", split_axis=0, concat_axis=0, tiled=True)
    slot_count = arrived.shape[1]
    grouped = arrived.reshape(exp_size, local_experts, slot_count, model_width)
    gate_up = jnp.einsum("seid,edf->seif", grouped, w_gate_up, preferred_element_type=jnp.float32)
    acted = (jax.nn.silu(gate_up[..., :FF]) * gate_up[..., FF:]).astype(jnp.bfloat16)
    produced = jnp.einsum(
        "seif,efd->seid", acted, w_down, preferred_element_type=jnp.float32
    ).astype(jnp.bfloat16)
    returned = lax.all_to_all(
        produced.reshape(expert_total, slot_count, model_width),
        "exp",
        split_axis=0,
        concat_axis=0,
        tiled=True,
    )
    selected = jnp.einsum(
        "tks,sd->tkd",
        picks.astype(jnp.bfloat16),
        returned.reshape(expert_total * capacity, model_width),
        preferred_element_type=jnp.float32,
    )
    weighted = jnp.sum(gate_weights[:, :, None] * selected, axis=1)
    return (hidden_f + weighted).astype(jnp.bfloat16)


MESH = pl.DeviceIdType.MESH
TOK = 128
ROWS = 256
GROUP = HQ // KVH
LOG2E = 1.4426950408889634
COLS = 512
ORDER = ((0, 0), (0, 1), (1, 0), (0, 2), (1, 1), (0, 3), (1, 2), (1, 3))


def layer_kernel(
    hid_ref, q_ref, k_ref, v_ref, blk_ref, list_ref, wo_ref, gain_ref, wgu_ref, wd_ref, ids_ref, gw_ref,
    out_ref,
    kv0, kv1, kcat, bias_s, q_s, att, wbuf, wgu_s, part_s, part_r, hid_s, nrm, act, ret_s, ret_r, g_s,
    loc_sem, own_sem, w_sem, zs, xs, cs, kv_recv, hs, hr, gs, gr, ps, pr, rs, rr,
):
    c = lax.axis_index("ctx")
    e = lax.axis_index("exp")
    z = c // 4
    x = (c // 2) % 2
    core = c % 2
    sibling = c + 1 - 2 * core
    x_peer = c + 2 - 4 * x
    kvs = (kv0, kv1)
    width = wo_ref.shape[1]
    chunks = width // COLS

    def kv_rows(block):
        return pl.ds(block * 2, 2)

    own_rows = kv_rows(c)
    mine = pl.ds(pl.multiple_of(e * TOK, TOK), TOK)
    other = pl.ds(pl.multiple_of((1 - e) * TOK, TOK), TOK)

    own = []
    for h in range(2):
        cols = pl.ds(pl.multiple_of(e * 2 * HD + h * HD, HD), HD)
        own.append(pltpu.make_async_copy(k_ref.at[:, :, cols], kvs[h].at[own_rows, :, pl.ds(0, HD)], own_sem.at[2 * h]))
        own.append(pltpu.make_async_copy(v_ref.at[:, :, cols], kvs[h].at[own_rows, :, pl.ds(HD, HD)], own_sem.at[2 * h + 1]))
    for copy in own:
        copy.start()
    q_copy = pltpu.make_async_copy(q_ref, q_s, loc_sem.at[0])
    hid_copy = pltpu.make_async_copy(hid_ref, hid_s.at[mine, :], loc_sem.at[1])
    wo_copy = pltpu.make_async_copy(wo_ref, wbuf.at[pl.ds(0, wo_ref.shape[0]), :], loc_sem.at[2])
    wd_copy = pltpu.make_async_copy(wd_ref, wbuf, loc_sem.at[3])
    wgu_copies = [pltpu.make_async_copy(wgu_ref.at[i], wgu_s.at[i], w_sem.at[i]) for i in range(4)]

    barrier = pltpu.get_barrier_semaphore()
    pl.semaphore_signal(barrier, inc=1, device_id=(sibling, e), device_id_type=MESH)
    pl.semaphore_signal(barrier, inc=1, device_id=(x_peer, e), device_id_type=MESH)
    pl.semaphore_signal(barrier, inc=1, device_id=(c, 1 - e), device_id_type=MESH)

    @pl.when(z > 0)
    def _():
        pl.semaphore_signal(barrier, inc=1, device_id=(c - 4, e), device_id_type=MESH)

    @pl.when(z < 3)
    def _():
        pl.semaphore_signal(barrier, inc=1, device_id=(c + 4, e), device_id_type=MESH)

    lane = lax.broadcasted_iota(jnp.int32, (TOK, HD), 1)
    g_s[mine, :] = jnp.where(lane == ids_ref[:, 0:1], gw_ref[:, 0:1], 0.0) + jnp.where(
        lane == ids_ref[:, 1:2], gw_ref[:, 1:2], 0.0
    )
    inner = (z > 0) & (z < 3)

    @pl.when(inner)
    def _():
        pl.semaphore_wait(barrier, 5)

    @pl.when(jnp.logical_not(inner))
    def _():
        pl.semaphore_wait(barrier, 4)

    def send(h, block, send_sem, device):
        rows = kv_rows(block)
        return pltpu.make_async_remote_copy(
            src_ref=kvs[h].at[rows], dst_ref=kvs[h].at[rows], send_sem=send_sem,
            recv_sem=kv_recv.at[h, block], device_id=(device, e), device_id_type=MESH,
        )

    def line(k):
        return (z - k) * 4 + x * 2 + core

    def across(k):
        return (z - k) * 4 + (1 - x) * 2 + core

    def z_send(h, k):
        return send(h, line(k), zs.at[h, k], c + 4)

    def x_send(h, k):
        return send(h, line(k), xs.at[h, k], x_peer)

    def c_send(h, k):
        return send(h, line(k), cs.at[h, k], sibling)

    def c_send_across(h, k):
        return send(h, across(k), cs.at[h, 4 + k], sibling)

    hid_send = pltpu.make_async_remote_copy(
        src_ref=hid_ref, dst_ref=hid_s.at[mine, :], send_sem=hs, recv_sem=hr,
        device_id=(c, 1 - e), device_id_type=MESH,
    )
    g_send = pltpu.make_async_remote_copy(
        src_ref=g_s.at[mine, :], dst_ref=g_s.at[mine, :], send_sem=gs, recv_sem=gr,
        device_id=(c, 1 - e), device_id_type=MESH,
    )

    def relay(h, k):
        @pl.when(z >= k)
        def _():
            if k > 0:
                send(h, line(k), zs.at[h, k], sibling).wait_recv()

            @pl.when(z < 3)
            def _():
                z_send(h, k).start()

            x_send(h, k).start()
            c_send(h, k).start()

    def relay_across(h, k):
        @pl.when(z >= k)
        def _():
            send(h, across(k), zs.at[h, k], sibling).wait_recv()
            c_send_across(h, k).start()

    for place, (h, k) in enumerate(ORDER):
        if k == 0:
            own[2 * h].wait()
            own[2 * h + 1].wait()
        relay(h, k)
        if place == 0:
            hid_send.start()
            g_send.start()
            q_copy.start()
            hid_copy.start()
            wo_copy.start()
            for copy in wgu_copies:
                copy.start()
        if place > 0:
            relay_across(*ORDER[place - 1])
    relay_across(*ORDER[-1])
    for h in range(2):
        for k in range(4):
            @pl.when(z >= k)
            def _(h=h, k=k):
                for xx in range(2):
                    send(h, (z - k) * 4 + xx * 2 + 1 - core, zs.at[h, k], sibling).wait_recv()
    q_copy.wait()

    scale = LOG2E / math.sqrt(HD)
    key_row = lax.broadcasted_iota(jnp.int32, (2 * BLK, BLK), 1)
    query_row = lax.broadcasted_iota(jnp.int32, (2 * BLK, BLK), 0) % BLK
    triangle = jnp.where(key_row <= query_row, 0.0, NEG_FILL).astype(jnp.float32)
    picks = blk_ref.shape[1]
    for t in range(2):
        for j in range(1, picks):
            listed = jnp.broadcast_to(list_ref[t : t + 1, j : j + 1], (1, BLK))
            again = jnp.zeros((1, BLK), jnp.float32)
            for i in range(j):
                again += jnp.where(listed == list_ref[t : t + 1, i : i + 1], 1.0, 0.0)
            bias_s[t, :, (j - 1) * BLK : j * BLK] = jnp.where(again > 0.0, NEG_FILL, 0.0)

    @pl.loop(0, 2)
    def _(t):
        rows = pl.ds(pl.multiple_of(t * BLK, BLK), BLK)
        listed = [blk_ref[t, j] for j in range(picks)]
        bias = bias_s[t]
        for h in range(2):
            for j in range(picks):
                kcat[j * BLK : (j + 1) * BLK, :] = kvs[h][listed[j]]

            @pl.loop(0, GROUP // 4)
            def _(quad):
                for half in range(2):
                    first = pl.multiple_of((h * GROUP + quad * 4 + half * 2) * HD, HD)
                    second = pl.multiple_of((h * GROUP + quad * 4 + half * 2 + 1) * HD, HD)
                    queries = jnp.concatenate([q_s[rows, pl.ds(first, HD)], q_s[rows, pl.ds(second, HD)]], axis=0)
                    scores = lax.dot_general(
                        queries, kcat[:, :HD], (((1,), (1,)), ((), ())), preferred_element_type=jnp.float32
                    )
                    near = scores[:, :BLK] * scale + triangle
                    far = scores[:, BLK:] * scale + bias
                    top = jnp.maximum(
                        jnp.max(near, axis=1, keepdims=True), jnp.max(far, axis=1, keepdims=True)
                    )
                    near = jnp.exp2(near - top)
                    far = jnp.exp2(far - top)
                    total = jnp.sum(near, axis=1, keepdims=True) + jnp.sum(far, axis=1, keepdims=True)
                    weights = jnp.concatenate([near.astype(jnp.bfloat16), far.astype(jnp.bfloat16)], axis=1)
                    mixed = jnp.dot(weights, kcat[:, HD:], preferred_element_type=jnp.float32) / total
                    mixed = mixed.astype(jnp.bfloat16)
                    att[rows, pl.ds(first, HD)] = mixed[:BLK]
                    att[rows, pl.ds(second, HD)] = mixed[BLK:]

    def chunk(n):
        return pl.ds(pl.multiple_of(n * COLS, COLS), COLS)

    def part_send(which, n):
        rows = mine if which == 0 else other
        return pltpu.make_async_remote_copy(
            src_ref=part_s.at[rows, chunk(n)], dst_ref=part_r.at[rows, chunk(n)], send_sem=ps.at[which, n],
            recv_sem=pr.at[which, n], device_id=(c, 1 - e), device_id_type=MESH,
        )

    def part_recv(which, n):
        rows = other if which == 0 else mine
        return pltpu.make_async_remote_copy(
            src_ref=part_s.at[rows, chunk(n)], dst_ref=part_r.at[rows, chunk(n)], send_sem=ps.at[which, n],
            recv_sem=pr.at[which, n], device_id=(c, 1 - e), device_id_type=MESH,
        )

    def ret_send(n):
        return pltpu.make_async_remote_copy(
            src_ref=ret_s.at[:, chunk(n)], dst_ref=ret_r.at[:, chunk(n)], send_sem=rs.at[n],
            recv_sem=rr.at[n], device_id=(c, 1 - e), device_id_type=MESH,
        )

    wo_copy.wait()
    depth = wo_ref.shape[0]

    @pl.loop(0, chunks)
    def _(n):
        product = jnp.dot(att[...], wbuf[:depth, chunk(n)], preferred_element_type=jnp.float32)
        part_s[:, chunk(n)] = product.astype(jnp.bfloat16)
        part_send(0, n).start()

    @pl.loop(0, chunks)
    def _(n):
        part_send(1, n).start()

    wd_copy.start()
    hid_copy.wait()
    hid_send.wait()
    g_send.wait()
    for copy in wgu_copies:
        copy.wait()

    for turn in range(2):
        rows = other if turn == 0 else mine

        @pl.loop(0, chunks)
        def _(n, turn=turn):
            part_recv(turn, n).wait_recv()

        hidden = (
            hid_s[rows, :].astype(jnp.float32)
            + (part_s[rows, :].astype(jnp.float32) + part_r[rows, :].astype(jnp.float32))
        ).astype(jnp.bfloat16)
        hid_s[rows, :] = hidden
        hidden_f = hidden.astype(jnp.float32)
        mean_square = jnp.mean(hidden_f * hidden_f, axis=1, keepdims=True)
        nrm[...] = (hidden_f * lax.rsqrt(mean_square + 1e-06) * gain_ref[...]).astype(jnp.bfloat16)

        @pl.loop(0, 4)
        def _(i):
            for n in range(FF // 256):
                gate = jnp.dot(
                    nrm[...], wgu_s[i, :, n * 256 : (n + 1) * 256], preferred_element_type=jnp.float32
                )
                up = jnp.dot(
                    nrm[...], wgu_s[i, :, FF + n * 256 : FF + (n + 1) * 256], preferred_element_type=jnp.float32
                )
                acted = gate / (1.0 + jnp.exp(-gate)) * up
                act[:, pl.ds(pl.multiple_of(i * FF + n * 256, 256), 256)] = acted.astype(jnp.bfloat16)

        if turn == 0:
            wd_copy.wait()
        gates = g_s[rows, :]
        shares = [
            jnp.sum(jnp.where(lane == e * 4 + i, gates, 0.0), axis=1, keepdims=True) for i in range(4)
        ]

        @pl.loop(0, chunks)
        def _(n, turn=turn, rows=rows, shares=shares):
            total = jnp.zeros((TOK, COLS), jnp.float32)
            for i in range(4):
                total += shares[i] * jnp.dot(
                    act[:, i * FF : (i + 1) * FF], wbuf[i * FF : (i + 1) * FF, chunk(n)],
                    preferred_element_type=jnp.float32,
                )
            if turn == 0:
                ret_s[:, chunk(n)] = total.astype(jnp.bfloat16)
                ret_send(n).start()
            else:
                ret_send(n).wait_recv()
                total += ret_r[:, chunk(n)].astype(jnp.float32)
                out_ref[:, chunk(n)] = (hid_s[rows, chunk(n)].astype(jnp.float32) + total).astype(jnp.bfloat16)

    @pl.loop(0, chunks)
    def _(n):
        part_send(0, n).wait_send()
        part_send(1, n).wait_send()
        ret_send(n).wait_send()

    for h in range(2):
        for k in range(4):
            @pl.when(z >= k)
            def _(h=h, k=k):
                @pl.when(z < 3)
                def _():
                    z_send(h, k).wait_send()

                x_send(h, k).wait_send()
                c_send(h, k).wait_send()
                c_send_across(h, k).wait_send()


def fused_body(
    hidden_in, queries, keys, values, blocks, out_weight, norm_gain, w_gate_up, w_down, expert_ids, gate_weights
):
    tokens, width = hidden_in.shape
    experts = w_gate_up.shape[0]
    seq = keys.shape[0] * lax.axis_size("ctx")
    bf16 = jnp.bfloat16
    dma = pltpu.SemaphoreType.DMA
    chunks = width // COLS
    hbm = pl.BlockSpec(memory_space=pl.ANY)
    vmem = pl.BlockSpec(memory_space=pltpu.VMEM)
    smem = pl.BlockSpec(memory_space=pltpu.SMEM)
    return pl.pallas_call(
        layer_kernel,
        out_shape=jax.ShapeDtypeStruct((tokens, width), bf16),
        in_specs=[hbm, hbm, hbm, hbm, smem, vmem, hbm, vmem, hbm, hbm, vmem, vmem],
        out_specs=vmem,
        scratch_shapes=[
            pltpu.VMEM((seq // BLK, BLK, 2 * HD), bf16),
            pltpu.VMEM((seq // BLK, BLK, 2 * HD), bf16),
            pltpu.VMEM((blocks.shape[1] * BLK, 2 * HD), bf16),
            pltpu.VMEM((2, 1, (blocks.shape[1] - 1) * BLK), jnp.float32),
            pltpu.VMEM(queries.shape, bf16),
            pltpu.VMEM(queries.shape, bf16),
            pltpu.VMEM((experts * FF, width), bf16),
            pltpu.VMEM(w_gate_up.shape, bf16),
            pltpu.VMEM((2 * tokens, width), bf16),
            pltpu.VMEM((2 * tokens, width), bf16),
            pltpu.VMEM((2 * tokens, width), bf16),
            pltpu.VMEM((tokens, width), bf16),
            pltpu.VMEM((tokens, experts * FF), bf16),
            pltpu.VMEM((tokens, width), bf16),
            pltpu.VMEM((tokens, width), bf16),
            pltpu.VMEM((2 * tokens, HD), jnp.float32),
            dma((4,)), dma((4,)), dma((4,)),
            dma((2, 4)), dma((2, 4)), dma((2, 8)), dma((2, 16)),
            dma, dma, dma, dma,
            dma((2, chunks)), dma((2, chunks)), dma((chunks,)), dma((chunks,)),
        ],
        compiler_params=pltpu.CompilerParams(
            collective_id=0, has_side_effects=True, vmem_limit_bytes=60 * 2**20
        ),
        cost_estimate=pl.CostEstimate(flops=14 * 10**9, bytes_accessed=5 * 10**7, transcendentals=5 * 10**6),
    )(
        hidden_in, queries, keys.reshape(2, BLK, -1), values.reshape(2, BLK, -1), blocks, blocks, out_weight,
        norm_gain.reshape(1, width),
        w_gate_up, w_down.reshape(experts * FF, width), expert_ids, gate_weights,
    )


def solution(mesh):
    fits = mesh.shape["ctx"] == 16 and mesh.shape["exp"] == 2
    return jax.shard_map(
        fused_body if fits else body,
        mesh=mesh,
        in_specs=(
            P(("ctx", "exp"), None),
            P("ctx", "exp"),
            P("ctx", None),
            P("ctx", None),
            P("ctx", None),
            P("exp", None),
            P(),
            P("exp", None, None),
            P("exp", None, None),
            P(("ctx", "exp"), None),
            P(("ctx", "exp"), None),
        ),
        out_specs=P(("ctx", "exp"), None),
        check_vma=False,
    )
```

```python
import math

import jax
import jax.numpy as jnp
from jax import lax
from jax.experimental import pallas as pl
from jax.experimental.pallas import tpu as pltpu
from jax.sharding import PartitionSpec as P

HQ = 32
KVH = 4
HD = 128
FF = 768
BLK = 128


NEG_FILL = -1e30


def shifted(value, axis, steps):
    count = lax.axis_size(axis)
    first, last = (max(0, -steps), min(count, count - steps))
    return lax.ppermute(value, axis, [(source, source + steps) for source in range(first, last)])


def body(
    hidden_in,
    queries,
    keys,
    values,
    blocks,
    out_weight,
    norm_gain,
    w_gate_up,
    w_down,
    expert_ids,
    gate_weights,
):
    query_len = queries.shape[0]
    local_heads = queries.shape[1] // HD
    head_group = HQ // KVH
    local_group = min(head_group, local_heads)
    kv_local = local_heads // local_group
    kv_width = kv_local * HD
    first_kv = lax.axis_index("exp") * local_heads // head_group
    kv_mine = jnp.concatenate(
        [
            lax.dynamic_slice_in_dim(keys, first_kv * HD, kv_width, 1),
            lax.dynamic_slice_in_dim(values, first_kv * HD, kv_width, 1),
        ],
        axis=1,
    )
    cycle_size = lax.axis_size("ctx")
    ctx_place = lax.axis_index("ctx")
    query_start = ctx_place * query_len
    score_scale = 1.0 / math.sqrt(HD)
    query_heads = queries.reshape(query_len, kv_local, local_group, HD)
    query_pos = query_start + jnp.arange(query_len, dtype=jnp.int32)
    query_tiles = blocks.shape[0]

    def update(state, key_part, value_part, live):
        running_max, weight_sum, accumulated = state
        row_count = key_part.shape[0]
        scores = (
            jnp.einsum(
                "skgd,tkd->skgt",
                query_heads,
                key_part.reshape(row_count, kv_local, HD),
                preferred_element_type=jnp.float32,
            )
            * score_scale
        )
        live_full = live[:, None, None, :]
        new_max = jnp.maximum(running_max, jnp.max(jnp.where(live_full, scores, NEG_FILL), axis=-1))
        weights = jnp.where(live_full, jnp.exp(scores - new_max[..., None]), 0.0)
        shrink = jnp.exp(running_max - new_max)
        weight_sum = weight_sum * shrink + jnp.sum(weights, axis=-1)
        product = jnp.einsum(
            "skgt,tkd->skgd",
            weights.astype(jnp.bfloat16),
            value_part.reshape(row_count, kv_local, HD),
            preferred_element_type=jnp.float32,
        )
        accumulated = accumulated * shrink[..., None] + product
        return (new_max, weight_sum, accumulated)

    def attend_block(state, kv_part, row_start):
        row_count = kv_part.shape[0]
        key_part = kv_part[:, :kv_width]
        value_part = kv_part[:, kv_width:]
        key_pos = row_start + jnp.arange(row_count, dtype=jnp.int32)
        listed = jnp.any(blocks[:, :, None] == (key_pos // BLK)[None, None, :], axis=1)
        listed_rows = jnp.broadcast_to(listed[:, None, :], (query_tiles, BLK, row_count)).reshape(
            query_len, row_count
        )
        live = listed_rows & (key_pos[None, :] <= query_pos[:, None])
        result_state = update(state, key_part, value_part, live)
        return result_state

    def attend(state, kv_part, row_start):
        row_count = kv_part.shape[0]
        return attend_block(state, kv_part, row_start)

    empty_state = (
        jnp.full((query_len, kv_local, local_group), NEG_FILL, jnp.float32),
        jnp.zeros((query_len, kv_local, local_group), jnp.float32),
        jnp.zeros((query_len, kv_local, local_group, HD), jnp.float32),
    )
    first_state = attend(empty_state, kv_mine, query_start)

    def cycle_turn(turn, carried):
        acc_state, travelling = carried
        travelling = shifted(travelling, "ctx", 1)
        source = (ctx_place - turn - 1) % cycle_size
        return (attend(acc_state, travelling, source * query_len), travelling)

    final_state, unused_kv = lax.fori_loop(0, cycle_size - 1, cycle_turn, (first_state, kv_mine))
    running_max, weight_sum, accumulated = final_state
    attended = (
        (accumulated / weight_sum[..., None])
        .astype(jnp.bfloat16)
        .reshape(query_len, local_heads * HD)
    )
    token_count = hidden_in.shape[0]
    mixed = lax.psum_scatter(
        jnp.dot(attended, out_weight, preferred_element_type=jnp.float32).astype(jnp.bfloat16),
        "exp",
        scatter_dimension=0,
        tiled=True,
    ).astype(jnp.float32)
    hidden = (hidden_in.astype(jnp.float32) + mixed).astype(jnp.bfloat16)
    hidden_f = lax.optimization_barrier(hidden).astype(jnp.float32)
    mean_square = jnp.mean(hidden_f * hidden_f, axis=-1, keepdims=True)
    normed = (hidden_f * lax.rsqrt(mean_square + 1e-06) * norm_gain).astype(jnp.bfloat16)
    exp_size = lax.axis_size("exp")
    local_experts = w_gate_up.shape[0]
    expert_total = local_experts * exp_size
    capacity = token_count // 2
    model_width = normed.shape[1]
    route_count = expert_ids.shape[1]
    flat_ids = expert_ids.reshape(token_count * route_count)
    flat_count = flat_ids.shape[0]
    order = jnp.arange(flat_count, dtype=jnp.int32)
    ahead = (flat_ids[:, None] == flat_ids[None, :]) & (order[None, :] < order[:, None])
    slot_rank = jnp.sum(ahead.astype(jnp.int32), axis=1)
    target = (flat_ids * capacity + slot_rank).reshape(token_count, route_count)
    slot_ids = jnp.arange(expert_total * capacity, dtype=jnp.int32)
    picks = target[:, :, None] == slot_ids[None, None, :]
    dispatch = jnp.any(picks, axis=1).astype(jnp.bfloat16)
    outgoing = (
        lax.dot_general(
            dispatch, normed, (((0,), (0,)), ((), ())), preferred_element_type=jnp.float32
        )
        .astype(jnp.bfloat16)
        .reshape(expert_total, capacity, model_width)
    )
    arrived = lax.all_to_all(outgoing, "exp", split_axis=0, concat_axis=0, tiled=True)
    slot_count = arrived.shape[1]
    grouped = arrived.reshape(exp_size, local_experts, slot_count, model_width)
    gate_up = jnp.einsum("seid,edf->seif", grouped, w_gate_up, preferred_element_type=jnp.float32)
    acted = (jax.nn.silu(gate_up[..., :FF]) * gate_up[..., FF:]).astype(jnp.bfloat16)
    produced = jnp.einsum(
        "seif,efd->seid", acted, w_down, preferred_element_type=jnp.float32
    ).astype(jnp.bfloat16)
    returned = lax.all_to_all(
        produced.reshape(expert_total, slot_count, model_width),
        "exp",
        split_axis=0,
        concat_axis=0,
        tiled=True,
    )
    selected = jnp.einsum(
        "tks,sd->tkd",
        picks.astype(jnp.bfloat16),
        returned.reshape(expert_total * capacity, model_width),
        preferred_element_type=jnp.float32,
    )
    weighted = jnp.sum(gate_weights[:, :, None] * selected, axis=1)
    return (hidden_f + weighted).astype(jnp.bfloat16)


MESH = pl.DeviceIdType.MESH
TOK = 128
ROWS = 256
GROUP = HQ // KVH
LOG2E = 1.4426950408889634
COLS = 512
ORDER = ((0, 0), (0, 1), (1, 0), (0, 2), (1, 1), (0, 3), (1, 2), (1, 3))


def layer_kernel(
    hid_ref, q_ref, k_ref, v_ref, blk_ref, list_ref, wo_ref, gain_ref, wgu_ref, wd_ref, ids_ref, gw_ref,
    out_ref,
    kv0, kv1, kcat, bias_s, q_s, att, wbuf, wgu_s, part_s, part_r, hid_s, nrm, act, ret_s, ret_r, g_s,
    loc_sem, own_sem, w_sem, zs, xs, cs, kv_recv, hs, hr, gs, gr, ps, pr, rs, rr,
):
    c = lax.axis_index("ctx")
    e = lax.axis_index("exp")
    z = c // 4
    x = (c // 2) % 2
    core = c % 2
    sibling = c + 1 - 2 * core
    x_peer = c + 2 - 4 * x
    kvs = (kv0, kv1)
    width = wo_ref.shape[1]
    chunks = width // COLS

    def kv_rows(block):
        return pl.ds(block * 2, 2)

    own_rows = kv_rows(c)
    mine = pl.ds(pl.multiple_of(e * TOK, TOK), TOK)
    other = pl.ds(pl.multiple_of((1 - e) * TOK, TOK), TOK)

    own = []
    for h in range(2):
        cols = pl.ds(pl.multiple_of(e * 2 * HD + h * HD, HD), HD)
        own.append(pltpu.make_async_copy(k_ref.at[:, :, cols], kvs[h].at[own_rows, :, pl.ds(0, HD)], own_sem.at[2 * h]))
        own.append(pltpu.make_async_copy(v_ref.at[:, :, cols], kvs[h].at[own_rows, :, pl.ds(HD, HD)], own_sem.at[2 * h + 1]))
    for copy in own:
        copy.start()
    q_copy = pltpu.make_async_copy(q_ref, q_s, loc_sem.at[0])
    hid_copy = pltpu.make_async_copy(hid_ref, hid_s.at[mine, :], loc_sem.at[1])
    wo_copy = pltpu.make_async_copy(wo_ref, wbuf.at[pl.ds(0, wo_ref.shape[0]), :], loc_sem.at[2])
    wd_copy = pltpu.make_async_copy(wd_ref, wbuf, loc_sem.at[3])
    wgu_copies = [pltpu.make_async_copy(wgu_ref.at[i], wgu_s.at[i], w_sem.at[i]) for i in range(4)]

    barrier = pltpu.get_barrier_semaphore()
    pl.semaphore_signal(barrier, inc=1, device_id=(sibling, e), device_id_type=MESH)
    pl.semaphore_signal(barrier, inc=1, device_id=(x_peer, e), device_id_type=MESH)
    pl.semaphore_signal(barrier, inc=1, device_id=(c, 1 - e), device_id_type=MESH)

    @pl.when(z > 0)
    def _():
        pl.semaphore_signal(barrier, inc=1, device_id=(c - 4, e), device_id_type=MESH)

    @pl.when(z < 3)
    def _():
        pl.semaphore_signal(barrier, inc=1, device_id=(c + 4, e), device_id_type=MESH)

    lane = lax.broadcasted_iota(jnp.int32, (TOK, HD), 1)
    g_s[mine, :] = jnp.where(lane == ids_ref[:, 0:1], gw_ref[:, 0:1], 0.0) + jnp.where(
        lane == ids_ref[:, 1:2], gw_ref[:, 1:2], 0.0
    )
    inner = (z > 0) & (z < 3)

    @pl.when(inner)
    def _():
        pl.semaphore_wait(barrier, 5)

    @pl.when(jnp.logical_not(inner))
    def _():
        pl.semaphore_wait(barrier, 4)

    def send(h, block, send_sem, device):
        rows = kv_rows(block)
        return pltpu.make_async_remote_copy(
            src_ref=kvs[h].at[rows], dst_ref=kvs[h].at[rows], send_sem=send_sem,
            recv_sem=kv_recv.at[h, block], device_id=(device, e), device_id_type=MESH,
        )

    def line(k):
        return (z - k) * 4 + x * 2 + core

    def across(k):
        return (z - k) * 4 + (1 - x) * 2 + core

    def z_send(h, k):
        return send(h, line(k), zs.at[h, k], c + 4)

    def x_send(h, k):
        return send(h, line(k), xs.at[h, k], x_peer)

    def c_send(h, k):
        return send(h, line(k), cs.at[h, k], sibling)

    def c_send_across(h, k):
        return send(h, across(k), cs.at[h, 4 + k], sibling)

    hid_send = pltpu.make_async_remote_copy(
        src_ref=hid_ref, dst_ref=hid_s.at[mine, :], send_sem=hs, recv_sem=hr,
        device_id=(c, 1 - e), device_id_type=MESH,
    )
    g_send = pltpu.make_async_remote_copy(
        src_ref=g_s.at[mine, :], dst_ref=g_s.at[mine, :], send_sem=gs, recv_sem=gr,
        device_id=(c, 1 - e), device_id_type=MESH,
    )

    def relay(h, k):
        @pl.when(z >= k)
        def _():
            if k > 0:
                send(h, line(k), zs.at[h, k], sibling).wait_recv()

            @pl.when(z < 3)
            def _():
                z_send(h, k).start()

            x_send(h, k).start()
            c_send(h, k).start()

    def relay_across(h, k):
        @pl.when(z >= k)
        def _():
            send(h, across(k), zs.at[h, k], sibling).wait_recv()
            c_send_across(h, k).start()

    for place, (h, k) in enumerate(ORDER[:-1]):
        if k == 0:
            own[2 * h].wait()
            own[2 * h + 1].wait()
        relay(h, k)
        if place == 0:
            hid_send.start()
            g_send.start()
            q_copy.start()
            hid_copy.start()
            wo_copy.start()
            for copy in wgu_copies:
                copy.start()
        if place > 0:
            relay_across(*ORDER[place - 1])

    def wait_sibling(h):
        for k in range(4):
            @pl.when(z >= k)
            def _(h=h, k=k):
                for xx in range(2):
                    send(h, (z - k) * 4 + xx * 2 + 1 - core, zs.at[h, k], sibling).wait_recv()

    scale = LOG2E / math.sqrt(HD)
    key_row = lax.broadcasted_iota(jnp.int32, (2 * BLK, BLK), 1)
    query_row = lax.broadcasted_iota(jnp.int32, (2 * BLK, BLK), 0) % BLK
    triangle = jnp.where(key_row <= query_row, 0.0, NEG_FILL).astype(jnp.float32)
    picks = blk_ref.shape[1]
    for t in range(2):
        for j in range(1, picks):
            listed = jnp.broadcast_to(list_ref[t : t + 1, j : j + 1], (1, BLK))
            again = jnp.zeros((1, BLK), jnp.float32)
            for i in range(j):
                again += jnp.where(listed == list_ref[t : t + 1, i : i + 1], 1.0, 0.0)
            bias_s[t, :, (j - 1) * BLK : j * BLK] = jnp.where(again > 0.0, NEG_FILL, 0.0)

    def attend(h, t):
        rows = pl.ds(pl.multiple_of(t * BLK, BLK), BLK)
        bias = bias_s[t]
        for j in range(picks):
            kcat[j * BLK : (j + 1) * BLK, :] = kvs[h][blk_ref[t, j]]

        @pl.loop(0, GROUP // 4)
        def _(quad):
            for half in range(2):
                first = pl.multiple_of((h * GROUP + quad * 4 + half * 2) * HD, HD)
                second = pl.multiple_of((h * GROUP + quad * 4 + half * 2 + 1) * HD, HD)
                queries = jnp.concatenate([q_s[rows, pl.ds(first, HD)], q_s[rows, pl.ds(second, HD)]], axis=0)
                scores = lax.dot_general(
                    queries, kcat[:, :HD], (((1,), (1,)), ((), ())), preferred_element_type=jnp.float32
                )
                near = scores[:, :BLK] * scale + triangle
                far = scores[:, BLK:] * scale + bias
                top = jnp.maximum(
                    jnp.max(near, axis=1, keepdims=True), jnp.max(far, axis=1, keepdims=True)
                )
                near = jnp.exp2(near - top)
                far = jnp.exp2(far - top)
                total = jnp.sum(near, axis=1, keepdims=True) + jnp.sum(far, axis=1, keepdims=True)
                weights = jnp.concatenate([near.astype(jnp.bfloat16), far.astype(jnp.bfloat16)], axis=1)
                mixed = jnp.dot(weights, kcat[:, HD:], preferred_element_type=jnp.float32) / total
                mixed = mixed.astype(jnp.bfloat16)
                att[rows, pl.ds(first, HD)] = mixed[:BLK]
                att[rows, pl.ds(second, HD)] = mixed[BLK:]

    def chunk(n):
        return pl.ds(pl.multiple_of(n * COLS, COLS), COLS)

    def part_send(which, n):
        rows = mine if which == 0 else other
        return pltpu.make_async_remote_copy(
            src_ref=part_s.at[rows, chunk(n)], dst_ref=part_r.at[rows, chunk(n)], send_sem=ps.at[which, n],
            recv_sem=pr.at[which, n], device_id=(c, 1 - e), device_id_type=MESH,
        )

    def part_recv(which, n):
        rows = other if which == 0 else mine
        return pltpu.make_async_remote_copy(
            src_ref=part_s.at[rows, chunk(n)], dst_ref=part_r.at[rows, chunk(n)], send_sem=ps.at[which, n],
            recv_sem=pr.at[which, n], device_id=(c, 1 - e), device_id_type=MESH,
        )

    def ret_send(n):
        return pltpu.make_async_remote_copy(
            src_ref=ret_s.at[:, chunk(n)], dst_ref=ret_r.at[:, chunk(n)], send_sem=rs.at[n],
            recv_sem=rr.at[n], device_id=(c, 1 - e), device_id_type=MESH,
        )

    depth = wo_ref.shape[0]

    def project(which):
        rows = mine if which == 0 else other

        @pl.loop(0, chunks)
        def _(n):
            product = jnp.dot(att[rows, :], wbuf[:depth, chunk(n)], preferred_element_type=jnp.float32)
            part_s[rows, chunk(n)] = product.astype(jnp.bfloat16)
            part_send(which, n).start()

    wait_sibling(0)
    q_copy.wait()
    attend(0, e)
    relay(*ORDER[-1])
    relay_across(*ORDER[-2])
    attend(0, 1 - e)
    relay_across(*ORDER[-1])
    wait_sibling(1)
    attend(1, e)
    wo_copy.wait()
    project(0)
    attend(1, 1 - e)
    project(1)

    wd_copy.start()
    hid_copy.wait()
    hid_send.wait()
    g_send.wait()
    for copy in wgu_copies:
        copy.wait()

    for turn in range(2):
        rows = other if turn == 0 else mine

        @pl.loop(0, chunks)
        def _(n, turn=turn):
            part_recv(turn, n).wait_recv()

        hidden = (
            hid_s[rows, :].astype(jnp.float32)
            + (part_s[rows, :].astype(jnp.float32) + part_r[rows, :].astype(jnp.float32))
        ).astype(jnp.bfloat16)
        hid_s[rows, :] = hidden
        hidden_f = hidden.astype(jnp.float32)
        mean_square = jnp.mean(hidden_f * hidden_f, axis=1, keepdims=True)
        nrm[...] = (hidden_f * lax.rsqrt(mean_square + 1e-06) * gain_ref[...]).astype(jnp.bfloat16)

        @pl.loop(0, 4)
        def _(i):
            for n in range(FF // 256):
                gate = jnp.dot(
                    nrm[...], wgu_s[i, :, n * 256 : (n + 1) * 256], preferred_element_type=jnp.float32
                )
                up = jnp.dot(
                    nrm[...], wgu_s[i, :, FF + n * 256 : FF + (n + 1) * 256], preferred_element_type=jnp.float32
                )
                acted = gate / (1.0 + jnp.exp(-gate)) * up
                act[:, pl.ds(pl.multiple_of(i * FF + n * 256, 256), 256)] = acted.astype(jnp.bfloat16)

        if turn == 0:
            wd_copy.wait()
        gates = g_s[rows, :]
        shares = [
            jnp.sum(jnp.where(lane == e * 4 + i, gates, 0.0), axis=1, keepdims=True) for i in range(4)
        ]

        @pl.loop(0, chunks)
        def _(n, turn=turn, rows=rows, shares=shares):
            total = jnp.zeros((TOK, COLS), jnp.float32)
            for i in range(4):
                total += shares[i] * jnp.dot(
                    act[:, i * FF : (i + 1) * FF], wbuf[i * FF : (i + 1) * FF, chunk(n)],
                    preferred_element_type=jnp.float32,
                )
            if turn == 0:
                ret_s[:, chunk(n)] = total.astype(jnp.bfloat16)
                ret_send(n).start()
            else:
                ret_send(n).wait_recv()
                total += ret_r[:, chunk(n)].astype(jnp.float32)
                out_ref[:, chunk(n)] = (hid_s[rows, chunk(n)].astype(jnp.float32) + total).astype(jnp.bfloat16)

    @pl.loop(0, chunks)
    def _(n):
        part_send(0, n).wait_send()
        part_send(1, n).wait_send()
        ret_send(n).wait_send()

    for h in range(2):
        for k in range(4):
            @pl.when(z >= k)
            def _(h=h, k=k):
                @pl.when(z < 3)
                def _():
                    z_send(h, k).wait_send()

                x_send(h, k).wait_send()
                c_send(h, k).wait_send()
                c_send_across(h, k).wait_send()


def fused_body(
    hidden_in, queries, keys, values, blocks, out_weight, norm_gain, w_gate_up, w_down, expert_ids, gate_weights
):
    tokens, width = hidden_in.shape
    experts = w_gate_up.shape[0]
    seq = keys.shape[0] * lax.axis_size("ctx")
    bf16 = jnp.bfloat16
    dma = pltpu.SemaphoreType.DMA
    chunks = width // COLS
    hbm = pl.BlockSpec(memory_space=pl.ANY)
    vmem = pl.BlockSpec(memory_space=pltpu.VMEM)
    smem = pl.BlockSpec(memory_space=pltpu.SMEM)
    return pl.pallas_call(
        layer_kernel,
        out_shape=jax.ShapeDtypeStruct((tokens, width), bf16),
        in_specs=[hbm, hbm, hbm, hbm, smem, vmem, hbm, vmem, hbm, hbm, vmem, vmem],
        out_specs=vmem,
        scratch_shapes=[
            pltpu.VMEM((seq // BLK, BLK, 2 * HD), bf16),
            pltpu.VMEM((seq // BLK, BLK, 2 * HD), bf16),
            pltpu.VMEM((blocks.shape[1] * BLK, 2 * HD), bf16),
            pltpu.VMEM((2, 1, (blocks.shape[1] - 1) * BLK), jnp.float32),
            pltpu.VMEM(queries.shape, bf16),
            pltpu.VMEM(queries.shape, bf16),
            pltpu.VMEM((experts * FF, width), bf16),
            pltpu.VMEM(w_gate_up.shape, bf16),
            pltpu.VMEM((2 * tokens, width), bf16),
            pltpu.VMEM((2 * tokens, width), bf16),
            pltpu.VMEM((2 * tokens, width), bf16),
            pltpu.VMEM((tokens, width), bf16),
            pltpu.VMEM((tokens, experts * FF), bf16),
            pltpu.VMEM((tokens, width), bf16),
            pltpu.VMEM((tokens, width), bf16),
            pltpu.VMEM((2 * tokens, HD), jnp.float32),
            dma((4,)), dma((4,)), dma((4,)),
            dma((2, 4)), dma((2, 4)), dma((2, 8)), dma((2, 16)),
            dma, dma, dma, dma,
            dma((2, chunks)), dma((2, chunks)), dma((chunks,)), dma((chunks,)),
        ],
        compiler_params=pltpu.CompilerParams(
            collective_id=0, has_side_effects=True, vmem_limit_bytes=60 * 2**20
        ),
        cost_estimate=pl.CostEstimate(flops=14 * 10**9, bytes_accessed=5 * 10**7, transcendentals=5 * 10**6),
    )(
        hidden_in, queries, keys.reshape(2, BLK, -1), values.reshape(2, BLK, -1), blocks, blocks, out_weight,
        norm_gain.reshape(1, width),
        w_gate_up, w_down.reshape(experts * FF, width), expert_ids, gate_weights,
    )


def solution(mesh):
    fits = mesh.shape["ctx"] == 16 and mesh.shape["exp"] == 2
    return jax.shard_map(
        fused_body if fits else body,
        mesh=mesh,
        in_specs=(
            P(("ctx", "exp"), None),
            P("ctx", "exp"),
            P("ctx", None),
            P("ctx", None),
            P("ctx", None),
            P("exp", None),
            P(),
            P("exp", None, None),
            P("exp", None, None),
            P(("ctx", "exp"), None),
            P(("ctx", "exp"), None),
        ),
        out_specs=P(("ctx", "exp"), None),
        check_vma=False,
    )
```

```python
import math

import jax
import jax.numpy as jnp
from jax import lax
from jax.experimental import pallas as pl
from jax.experimental.pallas import tpu as pltpu
from jax.sharding import PartitionSpec as P

HQ = 32
KVH = 4
HD = 128
FF = 768
BLK = 128


NEG_FILL = -1e30


def shifted(value, axis, steps):
    count = lax.axis_size(axis)
    first, last = (max(0, -steps), min(count, count - steps))
    return lax.ppermute(value, axis, [(source, source + steps) for source in range(first, last)])


def body(
    hidden_in,
    queries,
    keys,
    values,
    blocks,
    out_weight,
    norm_gain,
    w_gate_up,
    w_down,
    expert_ids,
    gate_weights,
):
    query_len = queries.shape[0]
    local_heads = queries.shape[1] // HD
    head_group = HQ // KVH
    local_group = min(head_group, local_heads)
    kv_local = local_heads // local_group
    kv_width = kv_local * HD
    first_kv = lax.axis_index("exp") * local_heads // head_group
    kv_mine = jnp.concatenate(
        [
            lax.dynamic_slice_in_dim(keys, first_kv * HD, kv_width, 1),
            lax.dynamic_slice_in_dim(values, first_kv * HD, kv_width, 1),
        ],
        axis=1,
    )
    cycle_size = lax.axis_size("ctx")
    ctx_place = lax.axis_index("ctx")
    query_start = ctx_place * query_len
    score_scale = 1.0 / math.sqrt(HD)
    query_heads = queries.reshape(query_len, kv_local, local_group, HD)
    query_pos = query_start + jnp.arange(query_len, dtype=jnp.int32)
    query_tiles = blocks.shape[0]

    def update(state, key_part, value_part, live):
        running_max, weight_sum, accumulated = state
        row_count = key_part.shape[0]
        scores = (
            jnp.einsum(
                "skgd,tkd->skgt",
                query_heads,
                key_part.reshape(row_count, kv_local, HD),
                preferred_element_type=jnp.float32,
            )
            * score_scale
        )
        live_full = live[:, None, None, :]
        new_max = jnp.maximum(running_max, jnp.max(jnp.where(live_full, scores, NEG_FILL), axis=-1))
        weights = jnp.where(live_full, jnp.exp(scores - new_max[..., None]), 0.0)
        shrink = jnp.exp(running_max - new_max)
        weight_sum = weight_sum * shrink + jnp.sum(weights, axis=-1)
        product = jnp.einsum(
            "skgt,tkd->skgd",
            weights.astype(jnp.bfloat16),
            value_part.reshape(row_count, kv_local, HD),
            preferred_element_type=jnp.float32,
        )
        accumulated = accumulated * shrink[..., None] + product
        return (new_max, weight_sum, accumulated)

    def attend_block(state, kv_part, row_start):
        row_count = kv_part.shape[0]
        key_part = kv_part[:, :kv_width]
        value_part = kv_part[:, kv_width:]
        key_pos = row_start + jnp.arange(row_count, dtype=jnp.int32)
        listed = jnp.any(blocks[:, :, None] == (key_pos // BLK)[None, None, :], axis=1)
        listed_rows = jnp.broadcast_to(listed[:, None, :], (query_tiles, BLK, row_count)).reshape(
            query_len, row_count
        )
        live = listed_rows & (key_pos[None, :] <= query_pos[:, None])
        result_state = update(state, key_part, value_part, live)
        return result_state

    def attend(state, kv_part, row_start):
        row_count = kv_part.shape[0]
        return attend_block(state, kv_part, row_start)

    empty_state = (
        jnp.full((query_len, kv_local, local_group), NEG_FILL, jnp.float32),
        jnp.zeros((query_len, kv_local, local_group), jnp.float32),
        jnp.zeros((query_len, kv_local, local_group, HD), jnp.float32),
    )
    first_state = attend(empty_state, kv_mine, query_start)

    def cycle_turn(turn, carried):
        acc_state, travelling = carried
        travelling = shifted(travelling, "ctx", 1)
        source = (ctx_place - turn - 1) % cycle_size
        return (attend(acc_state, travelling, source * query_len), travelling)

    final_state, unused_kv = lax.fori_loop(0, cycle_size - 1, cycle_turn, (first_state, kv_mine))
    running_max, weight_sum, accumulated = final_state
    attended = (
        (accumulated / weight_sum[..., None])
        .astype(jnp.bfloat16)
        .reshape(query_len, local_heads * HD)
    )
    token_count = hidden_in.shape[0]
    mixed = lax.psum_scatter(
        jnp.dot(attended, out_weight, preferred_element_type=jnp.float32).astype(jnp.bfloat16),
        "exp",
        scatter_dimension=0,
        tiled=True,
    ).astype(jnp.float32)
    hidden = (hidden_in.astype(jnp.float32) + mixed).astype(jnp.bfloat16)
    hidden_f = lax.optimization_barrier(hidden).astype(jnp.float32)
    mean_square = jnp.mean(hidden_f * hidden_f, axis=-1, keepdims=True)
    normed = (hidden_f * lax.rsqrt(mean_square + 1e-06) * norm_gain).astype(jnp.bfloat16)
    exp_size = lax.axis_size("exp")
    local_experts = w_gate_up.shape[0]
    expert_total = local_experts * exp_size
    capacity = token_count // 2
    model_width = normed.shape[1]
    route_count = expert_ids.shape[1]
    flat_ids = expert_ids.reshape(token_count * route_count)
    flat_count = flat_ids.shape[0]
    order = jnp.arange(flat_count, dtype=jnp.int32)
    ahead = (flat_ids[:, None] == flat_ids[None, :]) & (order[None, :] < order[:, None])
    slot_rank = jnp.sum(ahead.astype(jnp.int32), axis=1)
    target = (flat_ids * capacity + slot_rank).reshape(token_count, route_count)
    slot_ids = jnp.arange(expert_total * capacity, dtype=jnp.int32)
    picks = target[:, :, None] == slot_ids[None, None, :]
    dispatch = jnp.any(picks, axis=1).astype(jnp.bfloat16)
    outgoing = (
        lax.dot_general(
            dispatch, normed, (((0,), (0,)), ((), ())), preferred_element_type=jnp.float32
        )
        .astype(jnp.bfloat16)
        .reshape(expert_total, capacity, model_width)
    )
    arrived = lax.all_to_all(outgoing, "exp", split_axis=0, concat_axis=0, tiled=True)
    slot_count = arrived.shape[1]
    grouped = arrived.reshape(exp_size, local_experts, slot_count, model_width)
    gate_up = jnp.einsum("seid,edf->seif", grouped, w_gate_up, preferred_element_type=jnp.float32)
    acted = (jax.nn.silu(gate_up[..., :FF]) * gate_up[..., FF:]).astype(jnp.bfloat16)
    produced = jnp.einsum(
        "seif,efd->seid", acted, w_down, preferred_element_type=jnp.float32
    ).astype(jnp.bfloat16)
    returned = lax.all_to_all(
        produced.reshape(expert_total, slot_count, model_width),
        "exp",
        split_axis=0,
        concat_axis=0,
        tiled=True,
    )
    selected = jnp.einsum(
        "tks,sd->tkd",
        picks.astype(jnp.bfloat16),
        returned.reshape(expert_total * capacity, model_width),
        preferred_element_type=jnp.float32,
    )
    weighted = jnp.sum(gate_weights[:, :, None] * selected, axis=1)
    return (hidden_f + weighted).astype(jnp.bfloat16)


MESH = pl.DeviceIdType.MESH
TOK = 128
ROWS = 256
GROUP = HQ // KVH
LOG2E = 1.4426950408889634
COLS = 512
ORDER = ((0, 0), (0, 1), (1, 0), (0, 2), (1, 1), (0, 3), (1, 2), (1, 3))


def layer_kernel(
    hid_ref, q_ref, k_ref, v_ref, blk_ref, list_ref, wo_ref, gain_ref, wgu_ref, wd_ref, ids_ref, gw_ref,
    out_ref,
    kv0, kv1, kcat, bias_s, q_s, att, wbuf, wgu_s, part_s, part_r, hid_s, nrm, act, ret_s, ret_r, g_s,
    loc_sem, own_sem, w_sem, zs, xs, cs, kv_recv, hs, hr, gs, gr, ps, pr, rs, rr,
):
    c = lax.axis_index("ctx")
    e = lax.axis_index("exp")
    z = c // 4
    x = (c // 2) % 2
    core = c % 2
    sibling = c + 1 - 2 * core
    x_peer = c + 2 - 4 * x
    kvs = (kv0, kv1)
    width = wo_ref.shape[1]
    chunks = width // COLS

    def kv_rows(block):
        return pl.ds(block * 2, 2)

    own_rows = kv_rows(c)
    mine = pl.ds(pl.multiple_of(e * TOK, TOK), TOK)
    other = pl.ds(pl.multiple_of((1 - e) * TOK, TOK), TOK)

    own = []
    for h in range(2):
        cols = pl.ds(pl.multiple_of(e * 2 * HD + h * HD, HD), HD)
        own.append(pltpu.make_async_copy(k_ref.at[:, :, cols], kvs[h].at[own_rows, :, pl.ds(0, HD)], own_sem.at[2 * h]))
        own.append(pltpu.make_async_copy(v_ref.at[:, :, cols], kvs[h].at[own_rows, :, pl.ds(HD, HD)], own_sem.at[2 * h + 1]))
    for copy in own:
        copy.start()
    q_copy = pltpu.make_async_copy(q_ref, q_s, loc_sem.at[0])
    hid_copy = pltpu.make_async_copy(hid_ref, hid_s.at[mine, :], loc_sem.at[1])
    wo_copy = pltpu.make_async_copy(wo_ref, wbuf.at[pl.ds(0, wo_ref.shape[0]), :], loc_sem.at[2])
    wd_copy = pltpu.make_async_copy(wd_ref, wbuf, loc_sem.at[3])
    wgu_copies = [pltpu.make_async_copy(wgu_ref.at[i], wgu_s.at[i], w_sem.at[i]) for i in range(4)]

    barrier = pltpu.get_barrier_semaphore()
    pl.semaphore_signal(barrier, inc=1, device_id=(sibling, e), device_id_type=MESH)
    pl.semaphore_signal(barrier, inc=1, device_id=(x_peer, e), device_id_type=MESH)
    pl.semaphore_signal(barrier, inc=1, device_id=(c, 1 - e), device_id_type=MESH)

    @pl.when(z > 0)
    def _():
        pl.semaphore_signal(barrier, inc=1, device_id=(c - 4, e), device_id_type=MESH)

    @pl.when(z < 3)
    def _():
        pl.semaphore_signal(barrier, inc=1, device_id=(c + 4, e), device_id_type=MESH)

    lane = lax.broadcasted_iota(jnp.int32, (TOK, HD), 1)
    g_s[mine, :] = jnp.where(lane == ids_ref[:, 0:1], gw_ref[:, 0:1], 0.0) + jnp.where(
        lane == ids_ref[:, 1:2], gw_ref[:, 1:2], 0.0
    )
    inner = (z > 0) & (z < 3)

    @pl.when(inner)
    def _():
        pl.semaphore_wait(barrier, 5)

    @pl.when(jnp.logical_not(inner))
    def _():
        pl.semaphore_wait(barrier, 4)

    def send(h, block, send_sem, device):
        rows = kv_rows(block)
        return pltpu.make_async_remote_copy(
            src_ref=kvs[h].at[rows], dst_ref=kvs[h].at[rows], send_sem=send_sem,
            recv_sem=kv_recv.at[h, block], device_id=(device, e), device_id_type=MESH,
        )

    def line(k):
        return (z - k) * 4 + x * 2 + core

    def across(k):
        return (z - k) * 4 + (1 - x) * 2 + core

    def z_send(h, k):
        return send(h, line(k), zs.at[h, k], c + 4)

    def x_send(h, k):
        return send(h, line(k), xs.at[h, k], x_peer)

    def c_send(h, k):
        return send(h, line(k), cs.at[h, k], sibling)

    def c_send_across(h, k):
        return send(h, across(k), cs.at[h, 4 + k], sibling)

    hid_send = pltpu.make_async_remote_copy(
        src_ref=hid_ref, dst_ref=hid_s.at[mine, :], send_sem=hs, recv_sem=hr,
        device_id=(c, 1 - e), device_id_type=MESH,
    )
    g_send = pltpu.make_async_remote_copy(
        src_ref=g_s.at[mine, :], dst_ref=g_s.at[mine, :], send_sem=gs, recv_sem=gr,
        device_id=(c, 1 - e), device_id_type=MESH,
    )

    def relay(h, k):
        @pl.when(z >= k)
        def _():
            if k > 0:
                send(h, line(k), zs.at[h, k], sibling).wait_recv()

            @pl.when(z < 3)
            def _():
                z_send(h, k).start()

            x_send(h, k).start()
            c_send(h, k).start()

    def relay_across(h, k):
        @pl.when(z >= k)
        def _():
            send(h, across(k), zs.at[h, k], sibling).wait_recv()
            c_send_across(h, k).start()

    for place, (h, k) in enumerate(ORDER[:-1]):
        if k == 0:
            own[2 * h].wait()
            own[2 * h + 1].wait()
        relay(h, k)
        if place == 0:
            hid_send.start()
            g_send.start()
            q_copy.start()
            hid_copy.start()
            wo_copy.start()
            for copy in wgu_copies:
                copy.start()
        if place > 0:
            relay_across(*ORDER[place - 1])

    def wait_sibling(h):
        for k in range(4):
            @pl.when(z >= k)
            def _(h=h, k=k):
                for xx in range(2):
                    send(h, (z - k) * 4 + xx * 2 + 1 - core, zs.at[h, k], sibling).wait_recv()

    scale = LOG2E / math.sqrt(HD)
    key_row = lax.broadcasted_iota(jnp.int32, (2 * BLK, BLK), 1)
    query_row = lax.broadcasted_iota(jnp.int32, (2 * BLK, BLK), 0) % BLK
    triangle = jnp.where(key_row <= query_row, 0.0, NEG_FILL).astype(jnp.float32)
    picks = blk_ref.shape[1]
    for t in range(2):
        for j in range(1, picks):
            listed = jnp.broadcast_to(list_ref[t : t + 1, j : j + 1], (1, BLK))
            again = jnp.zeros((1, BLK), jnp.float32)
            for i in range(j):
                again += jnp.where(listed == list_ref[t : t + 1, i : i + 1], 1.0, 0.0)
            bias_s[t, :, (j - 1) * BLK : j * BLK] = jnp.where(again > 0.0, NEG_FILL, 0.0)

    def attend(h, t):
        rows = pl.ds(pl.multiple_of(t * BLK, BLK), BLK)
        bias = bias_s[t]
        for j in range(picks):
            kcat[j * BLK : (j + 1) * BLK, :] = kvs[h][blk_ref[t, j]]

        @pl.loop(0, GROUP // 4)
        def _(quad):
            for half in range(2):
                first = pl.multiple_of((h * GROUP + quad * 4 + half * 2) * HD, HD)
                second = pl.multiple_of((h * GROUP + quad * 4 + half * 2 + 1) * HD, HD)
                queries = jnp.concatenate([q_s[rows, pl.ds(first, HD)], q_s[rows, pl.ds(second, HD)]], axis=0)
                scores = lax.dot_general(
                    queries, kcat[:, :HD], (((1,), (1,)), ((), ())), preferred_element_type=jnp.float32
                )
                near = scores[:, :BLK] * scale + triangle
                far = scores[:, BLK:] * scale + bias
                top = jnp.maximum(
                    jnp.max(near, axis=1, keepdims=True), jnp.max(far, axis=1, keepdims=True)
                )
                near = jnp.exp2(near - top)
                far = jnp.exp2(far - top)
                total = jnp.sum(near, axis=1, keepdims=True) + jnp.sum(far, axis=1, keepdims=True)
                weights = jnp.concatenate([near.astype(jnp.bfloat16), far.astype(jnp.bfloat16)], axis=1)
                mixed = jnp.dot(weights, kcat[:, HD:], preferred_element_type=jnp.float32) / total
                mixed = mixed.astype(jnp.bfloat16)
                att[rows, pl.ds(first, HD)] = mixed[:BLK]
                att[rows, pl.ds(second, HD)] = mixed[BLK:]

    def chunk(n):
        return pl.ds(pl.multiple_of(n * COLS, COLS), COLS)

    def part_send(which, n):
        rows = mine if which == 0 else other
        return pltpu.make_async_remote_copy(
            src_ref=part_s.at[n, rows], dst_ref=part_r.at[n, rows], send_sem=ps.at[which, n],
            recv_sem=pr.at[which, n], device_id=(c, 1 - e), device_id_type=MESH,
        )

    def part_recv(which, n):
        rows = other if which == 0 else mine
        return pltpu.make_async_remote_copy(
            src_ref=part_s.at[n, rows], dst_ref=part_r.at[n, rows], send_sem=ps.at[which, n],
            recv_sem=pr.at[which, n], device_id=(c, 1 - e), device_id_type=MESH,
        )

    def ret_send(n):
        return pltpu.make_async_remote_copy(
            src_ref=ret_s.at[n], dst_ref=ret_r.at[n], send_sem=rs.at[n],
            recv_sem=rr.at[n], device_id=(c, 1 - e), device_id_type=MESH,
        )

    depth = wo_ref.shape[0]

    def project(which):
        rows = mine if which == 0 else other

        @pl.loop(0, chunks)
        def _(n):
            product = jnp.dot(att[rows, :], wbuf[:depth, chunk(n)], preferred_element_type=jnp.float32)
            part_s[n, rows, :] = product.astype(jnp.bfloat16)
            part_send(which, n).start()

    wait_sibling(0)
    q_copy.wait()
    attend(0, e)
    relay(*ORDER[-1])
    relay_across(*ORDER[-2])
    attend(0, 1 - e)
    relay_across(*ORDER[-1])
    wait_sibling(1)
    attend(1, e)
    wo_copy.wait()
    project(0)
    attend(1, 1 - e)
    project(1)

    wd_copy.start()
    hid_copy.wait()
    hid_send.wait()
    g_send.wait()
    for copy in wgu_copies:
        copy.wait()

    for turn in range(2):
        rows = other if turn == 0 else mine

        @pl.loop(0, chunks)
        def _(n, turn=turn):
            part_recv(turn, n).wait_recv()

        hidden = (
            hid_s[rows, :].astype(jnp.float32)
            + jnp.concatenate(
                [
                    part_s[n, rows, :].astype(jnp.float32) + part_r[n, rows, :].astype(jnp.float32)
                    for n in range(chunks)
                ],
                axis=1,
            )
        ).astype(jnp.bfloat16)
        hid_s[rows, :] = hidden
        hidden_f = hidden.astype(jnp.float32)
        mean_square = jnp.mean(hidden_f * hidden_f, axis=1, keepdims=True)
        nrm[...] = (hidden_f * lax.rsqrt(mean_square + 1e-06) * gain_ref[...]).astype(jnp.bfloat16)

        @pl.loop(0, 4)
        def _(i):
            for n in range(FF // 256):
                gate = jnp.dot(
                    nrm[...], wgu_s[i, :, n * 256 : (n + 1) * 256], preferred_element_type=jnp.float32
                )
                up = jnp.dot(
                    nrm[...], wgu_s[i, :, FF + n * 256 : FF + (n + 1) * 256], preferred_element_type=jnp.float32
                )
                acted = gate / (1.0 + jnp.exp(-gate)) * up
                act[:, pl.ds(pl.multiple_of(i * FF + n * 256, 256), 256)] = acted.astype(jnp.bfloat16)

        if turn == 0:
            wd_copy.wait()
        gates = g_s[rows, :]
        shares = [
            jnp.sum(jnp.where(lane == e * 4 + i, gates, 0.0), axis=1, keepdims=True) for i in range(4)
        ]

        @pl.loop(0, chunks)
        def _(n, turn=turn, rows=rows, shares=shares):
            total = jnp.zeros((TOK, COLS), jnp.float32)
            for i in range(4):
                total += shares[i] * jnp.dot(
                    act[:, i * FF : (i + 1) * FF], wbuf[i * FF : (i + 1) * FF, chunk(n)],
                    preferred_element_type=jnp.float32,
                )
            if turn == 0:
                ret_s[n] = total.astype(jnp.bfloat16)
                ret_send(n).start()
            else:
                ret_send(n).wait_recv()
                total += ret_r[n].astype(jnp.float32)
                out_ref[:, chunk(n)] = (hid_s[rows, chunk(n)].astype(jnp.float32) + total).astype(jnp.bfloat16)

    @pl.loop(0, chunks)
    def _(n):
        part_send(0, n).wait_send()
        part_send(1, n).wait_send()
        ret_send(n).wait_send()

    for h in range(2):
        for k in range(4):
            @pl.when(z >= k)
            def _(h=h, k=k):
                @pl.when(z < 3)
                def _():
                    z_send(h, k).wait_send()

                x_send(h, k).wait_send()
                c_send(h, k).wait_send()
                c_send_across(h, k).wait_send()


def fused_body(
    hidden_in, queries, keys, values, blocks, out_weight, norm_gain, w_gate_up, w_down, expert_ids, gate_weights
):
    tokens, width = hidden_in.shape
    experts = w_gate_up.shape[0]
    seq = keys.shape[0] * lax.axis_size("ctx")
    bf16 = jnp.bfloat16
    dma = pltpu.SemaphoreType.DMA
    chunks = width // COLS
    hbm = pl.BlockSpec(memory_space=pl.ANY)
    vmem = pl.BlockSpec(memory_space=pltpu.VMEM)
    smem = pl.BlockSpec(memory_space=pltpu.SMEM)
    return pl.pallas_call(
        layer_kernel,
        out_shape=jax.ShapeDtypeStruct((tokens, width), bf16),
        in_specs=[hbm, hbm, hbm, hbm, smem, vmem, hbm, vmem, hbm, hbm, vmem, vmem],
        out_specs=vmem,
        scratch_shapes=[
            pltpu.VMEM((seq // BLK, BLK, 2 * HD), bf16),
            pltpu.VMEM((seq // BLK, BLK, 2 * HD), bf16),
            pltpu.VMEM((blocks.shape[1] * BLK, 2 * HD), bf16),
            pltpu.VMEM((2, 1, (blocks.shape[1] - 1) * BLK), jnp.float32),
            pltpu.VMEM(queries.shape, bf16),
            pltpu.VMEM(queries.shape, bf16),
            pltpu.VMEM((experts * FF, width), bf16),
            pltpu.VMEM(w_gate_up.shape, bf16),
            pltpu.VMEM((chunks, 2 * tokens, COLS), bf16),
            pltpu.VMEM((chunks, 2 * tokens, COLS), bf16),
            pltpu.VMEM((2 * tokens, width), bf16),
            pltpu.VMEM((tokens, width), bf16),
            pltpu.VMEM((tokens, experts * FF), bf16),
            pltpu.VMEM((chunks, tokens, COLS), bf16),
            pltpu.VMEM((chunks, tokens, COLS), bf16),
            pltpu.VMEM((2 * tokens, HD), jnp.float32),
            dma((4,)), dma((4,)), dma((4,)),
            dma((2, 4)), dma((2, 4)), dma((2, 8)), dma((2, 16)),
            dma, dma, dma, dma,
            dma((2, chunks)), dma((2, chunks)), dma((chunks,)), dma((chunks,)),
        ],
        compiler_params=pltpu.CompilerParams(
            collective_id=0, has_side_effects=True, vmem_limit_bytes=60 * 2**20
        ),
        cost_estimate=pl.CostEstimate(flops=14 * 10**9, bytes_accessed=5 * 10**7, transcendentals=5 * 10**6),
    )(
        hidden_in, queries, keys.reshape(2, BLK, -1), values.reshape(2, BLK, -1), blocks, blocks, out_weight,
        norm_gain.reshape(1, width),
        w_gate_up, w_down.reshape(experts * FF, width), expert_ids, gate_weights,
    )


def solution(mesh):
    fits = mesh.shape["ctx"] == 16 and mesh.shape["exp"] == 2
    return jax.shard_map(
        fused_body if fits else body,
        mesh=mesh,
        in_specs=(
            P(("ctx", "exp"), None),
            P("ctx", "exp"),
            P("ctx", None),
            P("ctx", None),
            P("ctx", None),
            P("exp", None),
            P(),
            P("exp", None, None),
            P("exp", None, None),
            P(("ctx", "exp"), None),
            P(("ctx", "exp"), None),
        ),
        out_specs=P(("ctx", "exp"), None),
        check_vma=False,
    )
```
